32 devices in a mesh: row: 8 (over z, core), col: 4 (over y, x).
Axes of the slice: x: 2, y: 2, z: 4, core: 2. Of those that a mesh axis runs over, the one named last changes fastest.
Arguments:
- features: bfloat16 [4096, 256], P(('col', 'row')), may hold values from -6 to 6
- source_scale: float32 [4096], P(('col', 'row')), may hold values from 0.1 to 1
- target_scale: float32 [8192], P('row'), may hold values from 0.1 to 1
- weight: bfloat16 [256, 256], replicated, may hold values from -0.375 to 0.375
- cotangent: bfloat16 [8192, 256], P(('row', 'col')), may hold values from -6 to 6
- tile_src: int32 [64, 4, 8], P('row', 'col'), may hold values from 0 to 7, as said below
- tile_count: int32 [64, 4], P('row', 'col'), may hold values from 1 to 8, as said below
- edge_tgt: int32 [64, 4, 8, 32], P('row', 'col'), may hold values from 0 to 127
- edge_src: int32 [64, 4, 8, 32], P('row', 'col'), may hold values from 0 to 127
Outputs:
- activated: bfloat16 [8192, 256], P(('row', 'col'))
- weight_grad: float32 [256, 256], replicated
- feature_grad: bfloat16 [4096, 256], P(('col', 'row'))
The draws below stay inside these ranges and needn't reach their ends.
Inputs may be any that keep to these rules, and one draw needn't show every extreme that they name: `tile_src`: within one target block and one grid column the 8 slots name distinct source blocks of that column; slots at or past the block's count are unused. `tile_count`: some target block of some grid column uses all 8 slots in every draw.
All inputs are finite; a program needn't handle non-finite values.
Results may differ from the reference program's by a relative error of at most 0.018.
Values may be sent and summed in bfloat16 or wider, within the bound.
A program may use at most 64 MiB of HBM per device.

```python
import math
import jax
import jax.numpy as jnp
from jax import lax

B = 128
F = 256
TB = 8
KPT = 8
ET = 32
SB = 8
TBLK = 64
TNODES = 8192
SNODES = 4096
N_ROW = 8
N_COL = 4


def draw_tile_src(key, part):
    key = jax.random.fold_in(key, 11)
    keys = jax.random.split(key, TBLK * N_COL)
    picks = jax.vmap(lambda single: jax.random.permutation(single, SB)[:KPT])(keys)
    return picks.reshape(TBLK, N_COL, KPT).astype(jnp.int32)


def draw_tile_count(key, part):
    key = jax.random.fold_in(key, 23)
    first, second = jax.random.split(key)
    counts = jax.random.randint(first, (TBLK * N_COL,), 1, KPT + 1)
    where = jax.random.randint(second, (), 0, TBLK * N_COL)
    counts = counts.at[where].set(KPT)
    return counts.reshape(TBLK, N_COL).astype(jnp.int32)


def touch_ends(array, key, smallest, largest):
    index_at = [jax.random.randint(jax.random.fold_in(key, axis), (), 0, length) for axis, length in enumerate(array.shape)]
    longest = array.shape.index(max(array.shape))
    next_to = index_at[:longest] + [(index_at[longest] + 1) % array.shape[longest]] + index_at[longest + 1:]
    return array.at[tuple(index_at)].set(smallest).at[tuple(next_to)].set(largest)


def level_of(key, shape, shards, least, high):
    def one(position, parts):
        draws = jax.random.uniform(jax.random.fold_in(jax.random.fold_in(key, 6), position), (parts,), jnp.float32, least / len(shards), high / len(shards))
        return jnp.repeat(jnp.exp(draws), shape[position] // parts).reshape((-1,) + (1,) * (len(shape) - position - 1))

    loudness = one(*shards[0])
    for cut in shards[1:]:
        loudness = loudness * one(*cut)
    return loudness


def gaussian(rng, extent, width, limit, shards=(), kind=jnp.bfloat16):
    result = jax.random.normal(rng, extent, jnp.float32) * width
    if len(shards) > 0:
        result = level_of(rng, extent, shards, -0.22, 0.18) * result
    return jnp.clip(result, min=-limit, max=limit).astype(kind)


def setup_inputs(seed: int = 0) -> dict:
    key_list = jax.random.split(jax.random.key(seed), 10)
    features = gaussian(key_list[0], (SNODES, F), 1.0, 6.0, ((0, 32),))
    source_scale = jnp.clip(jnp.exp(math.log(1.0) - 2.3025851 * jax.random.uniform(key_list[1], (SNODES,), jnp.float32) ** level_of(key_list[1], (SNODES,), ((0, 32),), -0.2, 0.2)), 0.1, 1.0)
    target_scale = jnp.clip(jnp.exp(math.log(1.0) - 2.3025851 * jax.random.uniform(key_list[2], (TNODES,), jnp.float32) ** level_of(key_list[2], (TNODES,), ((0, 8),), -0.2, 0.2)), 0.1, 1.0)
    weight = gaussian(key_list[3], (F, F), F ** -0.5, 0.375)
    cotangent = gaussian(key_list[4], (TNODES, F), 1.0, 6.0, ((0, 32),))
    tile_src = draw_tile_src(jax.random.fold_in(key_list[9], 71), 0)
    tile_count = draw_tile_count(jax.random.fold_in(key_list[9], 71), 0)
    edge_tgt = touch_ends(jax.random.randint(key_list[7], (TBLK, N_COL, KPT, ET), 0, B), jax.random.fold_in(key_list[7], 1), 0, B - 1).astype(jnp.int32)
    edge_src = touch_ends(jax.random.randint(key_list[8], (TBLK, N_COL, KPT, ET), 0, B), jax.random.fold_in(key_list[8], 1), 0, B - 1).astype(jnp.int32)
    return dict(features=features, source_scale=source_scale, target_scale=target_scale, weight=weight, cotangent=cotangent, tile_src=tile_src, tile_count=tile_count, edge_tgt=edge_tgt, edge_src=edge_src)


def reference(features, source_scale, target_scale, weight, cotangent, tile_src, tile_count, edge_tgt, edge_src):
    scaled = (source_scale[:, None] * features.astype(jnp.float32)).astype(jnp.bfloat16)
    groups = scaled.reshape(N_COL, SB * B, F)
    slot_ids = jnp.arange(KPT, dtype=jnp.int32)
    alive = slot_ids[None, None, :] < tile_count[:, :, None]
    columns = jnp.arange(N_COL, dtype=jnp.int32)

    def forward_block(item):
        slots, living, targets, sources = item
        rows = (slots[:, :, None] * B + sources).astype(jnp.int32)
        values = groups[columns[:, None, None], rows].astype(jnp.float32)
        values = jnp.where(living[:, :, None, None], values, jnp.float32(0.0))
        total = jnp.zeros((B, F), jnp.float32)
        return total.at[targets.reshape(-1)].add(values.reshape(-1, F))
    sums = lax.map(forward_block, (tile_src, alive, edge_tgt, edge_src))
    aggregated = (target_scale[:, None] * sums.reshape(TNODES, F)).astype(jnp.bfloat16)
    z_value = jnp.dot(aggregated, weight, preferred_element_type=jnp.float32)
    sigma = jax.nn.sigmoid(z_value)
    activated = (z_value * sigma).astype(jnp.bfloat16)
    deriv = sigma * (1.0 + z_value * (1.0 - sigma))
    grad_z = (cotangent.astype(jnp.float32) * deriv).astype(jnp.bfloat16)
    weight_grad = jnp.dot(aggregated.T, grad_z, preferred_element_type=jnp.float32) / math.sqrt(TNODES)
    grad_y = (target_scale[:, None] * jnp.dot(grad_z, weight.T, preferred_element_type=jnp.float32)).astype(jnp.bfloat16)
    grad_y = grad_y.reshape(N_ROW, TB, B, F)
    src_rows = tile_src.reshape(N_ROW, TB, N_COL, KPT)
    live_rows = alive.reshape(N_ROW, TB, N_COL, KPT)
    tgt_rows = edge_tgt.reshape(N_ROW, TB, N_COL, KPT, ET)
    srce_rows = edge_src.reshape(N_ROW, TB, N_COL, KPT, ET)
    block_ids = jnp.arange(TB, dtype=jnp.int32)

    def backward_column(column):

        def device_row(carry, grid_row):
            slots = src_rows[grid_row, :, column]
            living = live_rows[grid_row, :, column]
            targets = tgt_rows[grid_row, :, column]
            sources = srce_rows[grid_row, :, column]
            values = grad_y[grid_row][block_ids[:, None, None], targets].astype(jnp.float32)
            values = jnp.where(living[:, :, None, None], values, jnp.float32(0.0))
            dest = (slots[:, :, None] * B + sources).astype(jnp.int32)
            partial_value = jnp.zeros((SB * B, F), jnp.float32).at[dest.reshape(-1)].add(values.reshape(-1, F))
            rounded = lax.optimization_barrier(partial_value.astype(jnp.bfloat16))
            return (carry + rounded.astype(jnp.float32), None)
        total, unused = lax.scan(device_row, jnp.zeros((SB * B, F), jnp.float32), jnp.arange(N_ROW, dtype=jnp.int32))
        return total
    grads = lax.map(backward_column, columns)
    feature_grad = (source_scale[:, None] * grads.reshape(SNODES, F)).astype(jnp.bfloat16)
    return (activated, weight_grad, feature_grad)
```

```python
import functools
import math

import jax
import jax.numpy as jnp
from jax import lax
from jax.experimental import pallas as pl
from jax.experimental.pallas import tpu as pltpu
from jax.sharding import PartitionSpec as P

B = 128
BF = jnp.bfloat16
F32 = jnp.float32
NN = (((1,), (0,)), ((), ()))
NT = (((1,), (1,)), ((), ()))
TN = (((0,), (0,)), ((), ()))


def dot(left, right, dims=NN):
    return lax.dot_general(left, right, dims, preferred_element_type=F32)


def each(first, last, body):
    if last - first <= 8:
        for index in range(first, last):
            body(index)
    else:
        lax.fori_loop(first, last, lambda index, carry: (body(index), carry)[1], 0)


def rows_at(index, size):
    return pl.ds(pl.multiple_of(index * size, size), size)


def to_column(row_of, parts, offset, rows):
    place = lax.broadcasted_iota(jnp.int32, (rows, B), 0) + offset
    lane = lax.broadcasted_iota(jnp.int32, (rows, B), 1)
    picked = jnp.zeros((rows, B), F32)
    for part in range(parts):
        picked = picked + jnp.where(lane + part * B == place, row_of(part), 0.0)
    return jnp.sum(picked, axis=1, keepdims=True)


def kernel(
    n_row,
    n_col,
    total_nodes,
    feat_ref,
    sscale_ref,
    tscale_ref,
    weight_ref,
    cot_ref,
    slot_ref,
    count_ref,
    tgt_ref,
    src_ref,
    act_ref,
    wgrad_ref,
    fgrad_ref,
    gath,
    adj,
    adj_t,
    edges,
    part_send,
    part_recv,
    gy,
    f_send,
    f_recv,
    w_send,
    w_recv,
    x_send,
    x_recv,
    w_all,
    g_ss,
    g_rs,
    p_ss,
    p_rs,
    y_ss,
    y_rs,
    f_ss,
    f_rs,
    w_ss,
    w_rs,
    x_ss,
    x_rs,
    o_ss,
    o_rs,
):
    row = lax.axis_index("row")
    col = lax.axis_index("col")
    own, width = feat_ref.shape
    share = cot_ref.shape[0]
    blocks, slots, entries = tgt_ref.shape
    per_block = slots * entries
    src_blocks = n_row * own // B
    chunk = weight_ref.shape[0] // n_row

    def row_peer(step):
        return lax.rem(row + step, n_row)

    def col_peer(step):
        return lax.rem(col + step, n_col)

    barrier = pltpu.get_barrier_semaphore()

    def greet_row(step):
        pl.semaphore_signal(
            barrier, 1, device_id=(row_peer(step), col), device_id_type=pl.DeviceIdType.MESH
        )

    def greet_col(step):
        pl.semaphore_signal(
            barrier, 1, device_id=(row, col_peer(step)), device_id_type=pl.DeviceIdType.MESH
        )

    each(1, n_row, greet_row)
    each(1, n_col, greet_col)

    def row_copy(source, target, send_sem, recv_sem, peer, at):
        return pltpu.make_async_remote_copy(
            src_ref=source,
            dst_ref=target.at[at],
            send_sem=send_sem.at[peer],
            recv_sem=recv_sem.at[at],
            device_id=(peer, col),
            device_id_type=pl.DeviceIdType.MESH,
        )

    def col_copy(source, target, send_sem, recv_sem, peer, at):
        return pltpu.make_async_remote_copy(
            src_ref=source,
            dst_ref=target.at[at],
            send_sem=send_sem.at[peer],
            recv_sem=recv_sem.at[at],
            device_id=(row, peer),
            device_id_type=pl.DeviceIdType.MESH,
        )

    source_col = to_column(lambda part: sscale_ref[pl.ds(part, 1), :], own // B, 0, own)
    gath[row] = (source_col * feat_ref[...].astype(F32)).astype(BF)
    pl.semaphore_wait(barrier, n_row + n_col - 2)

    def send_feat(step):
        row_copy(gath.at[row], gath, g_ss, g_rs, row_peer(step), row).start()

    each(1, n_row, send_feat)

    lane = lax.broadcasted_iota(jnp.int32, (entries, per_block), 1)
    spread = (lane % entries == lax.broadcasted_iota(jnp.int32, (entries, per_block), 0)).astype(
        F32
    ).astype(BF)
    slot_lane = lax.broadcasted_iota(jnp.int32, (slots, per_block), 1) // entries
    slot_hot = slot_lane == lax.broadcasted_iota(jnp.int32, (slots, per_block), 0)

    def flatten(ref):
        flat = ref[...].reshape(blocks * slots, entries).astype(F32).astype(BF)
        wide = dot(flat, spread).reshape(blocks, slots, per_block)
        return jnp.sum(jnp.where(slot_hot[None], wide, 0.0), axis=1)

    block_lane = lax.broadcasted_iota(jnp.int32, (blocks, per_block), 1) // entries
    alive = block_lane < count_ref[...]
    edges[0] = jnp.where(alive, flatten(tgt_ref), -1.0)
    edges[1] = flatten(src_ref)
    edges[2] = dot(slot_ref[...].astype(F32).astype(BF), slot_hot.astype(F32).astype(BF))

    place = lax.broadcasted_iota(jnp.int32, (B, per_block), 0).astype(F32)

    def fill(block, carry):
        target_hot = (place == edges[0, pl.ds(block, 1), :]).astype(F32).astype(BF)
        source_hot = (place == edges[1, pl.ds(block, 1), :]).astype(F32).astype(BF)
        slot_row = edges[2, pl.ds(block, 1), :]
        step = min(8, src_blocks)
        for begin in range(0, src_blocks, step):
            parts = []
            for source in range(begin, begin + step):
                here = (slot_row == float(source)).astype(F32).astype(BF)
                parts.append(source_hot * here)
            placed = jnp.concatenate(parts, axis=0)
            span = pl.ds(begin * B, step * B)
            adj[rows_at(block, B), span] = dot(target_hot, placed, NT).astype(BF)
            adj_t[span, rows_at(block, B)] = dot(placed, target_hot, NT).astype(BF)
        return carry

    lax.fori_loop(0, blocks, fill, 0)

    offset = col * share
    scale_share = to_column(
        lambda part: tscale_ref[pl.ds(part, 1), :], blocks, offset, share
    )

    def wait_feat(step):
        peer = row_peer(step)
        row_copy(gath.at[row], gath, g_ss, g_rs, peer, peer).wait()

    each(1, n_row, wait_feat)
    gathered = gath[...].reshape(n_row * own, width)

    def send_part(step):
        peer = col_peer(step)
        part_send[peer] = dot(adj[rows_at(peer, share), :], gathered).astype(BF)
        col_copy(part_send.at[peer], part_recv, p_ss, p_rs, peer, col).start()

    each(1, n_col, send_part)
    part_recv[col] = dot(adj[rows_at(col, share), :], gathered).astype(BF)

    def wait_part(step):
        peer = col_peer(step)
        col_copy(part_send.at[peer], part_recv, p_ss, p_rs, peer, peer).wait()

    each(1, n_col, wait_part)
    summed = jnp.sum(part_recv[...].astype(F32), axis=0)
    agg = (scale_share * summed).astype(BF)
    z_value = dot(agg, weight_ref[...])
    sigma = jax.nn.sigmoid(z_value)
    deriv = sigma * (1.0 + z_value * (1.0 - sigma))
    grad = (cot_ref[...].astype(F32) * deriv).astype(BF)
    gy[col] = (scale_share * dot(grad, weight_ref[...], NT)).astype(BF)

    def send_gy(step):
        col_copy(gy.at[col], gy, y_ss, y_rs, col_peer(step), col).start()

    each(1, n_col, send_gy)
    w_send[...] = dot(agg, grad, TN).reshape(n_row, chunk, width).astype(w_send.dtype)

    def send_w(step):
        peer = row_peer(step)
        row_copy(w_send.at[peer], w_recv, w_ss, w_rs, peer, row).start()

    each(1, n_row, send_w)
    w_recv[row] = w_send[row]
    act_ref[...] = (z_value * sigma).astype(BF)

    def wait_gy(step):
        peer = col_peer(step)
        col_copy(gy.at[col], gy, y_ss, y_rs, peer, peer).wait()

    def wait_w(step):
        peer = row_peer(step)
        row_copy(w_send.at[peer], w_recv, w_ss, w_rs, peer, peer).wait()

    each(1, n_row, wait_w)
    x_recv[col] = jnp.sum(w_recv[...].astype(F32), axis=0).astype(x_recv.dtype)

    def send_x(step):
        col_copy(x_recv.at[col], x_recv, x_ss, x_rs, col_peer(step), col).start()

    each(1, n_col, send_x)
    each(1, n_col, wait_gy)
    grad_y = gy[...].reshape(n_col * share, width)

    def send_f(step):
        peer = row_peer(step)
        f_send[peer] = dot(adj_t[rows_at(peer, own), :], grad_y).astype(BF)
        row_copy(f_send.at[peer], f_recv, f_ss, f_rs, peer, row).start()

    each(1, n_row, send_f)
    f_recv[row] = dot(adj_t[rows_at(row, own), :], grad_y).astype(BF)

    def wait_x(step):
        peer = col_peer(step)
        col_copy(x_recv.at[col], x_recv, x_ss, x_rs, peer, peer).wait()

    each(1, n_col, wait_x)
    w_all[row] = (
        jnp.sum(x_recv[...].astype(F32), axis=0) * (1.0 / math.sqrt(total_nodes))
    ).astype(w_all.dtype)

    def send_o(step):
        row_copy(w_all.at[row], w_all, o_ss, o_rs, row_peer(step), row).start()

    each(1, n_row, send_o)

    def wait_f(step):
        peer = row_peer(step)
        row_copy(f_send.at[peer], f_recv, f_ss, f_rs, peer, peer).wait()

    each(1, n_row, wait_f)
    fgrad_ref[...] = (source_col * jnp.sum(f_recv[...].astype(F32), axis=0)).astype(BF)

    def wait_o(step):
        peer = row_peer(step)
        row_copy(w_all.at[row], w_all, o_ss, o_rs, peer, peer).wait()

    each(1, n_row, wait_o)
    wgrad_ref[...] = w_all[...].astype(F32).reshape(wgrad_ref.shape)


def on_device(
    features,
    source_scale,
    target_scale,
    weight,
    cotangent,
    tile_src,
    tile_count,
    edge_tgt,
    edge_src,
    n_row,
    n_col,
):
    own, width = features.shape
    share = cotangent.shape[0]
    blocks, _, slots, entries = edge_tgt.shape
    targets = blocks * B
    sources = own * n_row
    chunk = width // n_row
    wtype = BF if chunk % 16 == 0 else F32
    vmem = pl.BlockSpec(memory_space=pltpu.VMEM)
    dma = pltpu.SemaphoreType.DMA
    row_sem, col_sem = dma((n_row,)), dma((n_col,))
    return pl.pallas_call(
        functools.partial(kernel, n_row, n_col, targets * n_row),
        out_shape=(
            jax.ShapeDtypeStruct((share, width), BF),
            jax.ShapeDtypeStruct((width, width), F32),
            jax.ShapeDtypeStruct((own, width), BF),
        ),
        in_specs=[vmem] * 9,
        out_specs=(vmem,) * 3,
        scratch_shapes=[
            pltpu.VMEM((n_row, own, width), BF),
            pltpu.VMEM((targets, sources), BF),
            pltpu.VMEM((sources, targets), BF),
            pltpu.VMEM((3, blocks, slots * entries), F32),
            pltpu.VMEM((n_col, share, width), BF),
            pltpu.VMEM((n_col, share, width), BF),
            pltpu.VMEM((n_col, share, width), BF),
            pltpu.VMEM((n_row, own, width), BF),
            pltpu.VMEM((n_row, own, width), BF),
            pltpu.VMEM((n_row, chunk, width), wtype),
            pltpu.VMEM((n_row, chunk, width), wtype),
            pltpu.VMEM((n_col, chunk, width), wtype),
            pltpu.VMEM((n_col, chunk, width), wtype),
            pltpu.VMEM((n_row, chunk, width), wtype),
            row_sem,
            row_sem,
            col_sem,
            col_sem,
            col_sem,
            col_sem,
            row_sem,
            row_sem,
            row_sem,
            row_sem,
            col_sem,
            col_sem,
            row_sem,
            row_sem,
        ],
        compiler_params=pltpu.CompilerParams(
            collective_id=0, has_side_effects=True, vmem_limit_bytes=48 * 1024 * 1024
        ),
        cost_estimate=pl.CostEstimate(
            flops=4 * targets * sources * width,
            bytes_accessed=4 * sources * width,
            transcendentals=share * width,
        ),
    )(
        features,
        source_scale.reshape(own // B, B),
        target_scale.reshape(blocks, B),
        weight,
        cotangent,
        tile_src[:, 0],
        tile_count,
        edge_tgt[:, 0],
        edge_src[:, 0],
    )


def solution(mesh):
    in_specs = (
        P(("col", "row"), None),
        P(("col", "row")),
        P("row"),
        P(),
        P(("row", "col"), None),
        P("row", "col", None),
        P("row", "col"),
        P("row", "col", None, None),
        P("row", "col", None, None),
    )
    out_specs = (P(("row", "col"), None), P(), P(("col", "row"), None))
    body = functools.partial(on_device, n_row=mesh.shape["row"], n_col=mesh.shape["col"])
    return jax.shard_map(
        body, mesh=mesh, in_specs=in_specs, out_specs=out_specs, check_vma=False
    )
```

```python
import functools
import math

import jax
import jax.numpy as jnp
from jax import lax
from jax.experimental import pallas as pl
from jax.experimental.pallas import tpu as pltpu
from jax.sharding import PartitionSpec as P

B = 128
BF = jnp.bfloat16
F32 = jnp.float32
NN = (((1,), (0,)), ((), ()))
NT = (((1,), (1,)), ((), ()))
TN = (((0,), (0,)), ((), ()))


def dot(left, right, dims=NN):
    return lax.dot_general(left, right, dims, preferred_element_type=F32)


def each(first, last, body):
    if last - first <= 8:
        for index in range(first, last):
            body(index)
    else:
        lax.fori_loop(first, last, lambda index, carry: (body(index), carry)[1], 0)


def rows_at(index, size):
    return pl.ds(pl.multiple_of(index * size, size), size)


def to_column(row_of, parts, offset, rows):
    place = lax.broadcasted_iota(jnp.int32, (rows, B), 0) + offset
    lane = lax.broadcasted_iota(jnp.int32, (rows, B), 1)
    picked = jnp.zeros((rows, B), F32)
    for part in range(parts):
        picked = picked + jnp.where(lane + part * B == place, row_of(part), 0.0)
    return jnp.sum(picked, axis=1, keepdims=True)


def kernel(
    n_row,
    n_col,
    total_nodes,
    feat_hbm,
    sscale_hbm,
    tscale_hbm,
    weight_hbm,
    cot_hbm,
    slot_hbm,
    count_hbm,
    tgt_hbm,
    src_hbm,
    act_ref,
    wgrad_ref,
    fgrad_ref,
    feat_ref,
    sscale_ref,
    tscale_ref,
    weight_ref,
    cot_ref,
    slot_ref,
    count_ref,
    tgt_ref,
    src_ref,
    gath,
    adj,
    adj_t,
    edges,
    part_send,
    part_recv,
    agg,
    gy,
    f_pair,
    f_got,
    f_send,
    f_recv,
    w_pair,
    w_got,
    w_send,
    w_recv,
    x_all,
    w_all,
    in_sem,
    g_ss,
    g_rs,
    gp_ss,
    gp_rs,
    p_ss,
    p_rs,
    y_ss,
    y_rs,
    fp_ss,
    fp_rs,
    f_ss,
    f_rs,
    wp_ss,
    wp_rs,
    w_ss,
    w_rs,
    x_ss,
    x_rs,
    o_ss,
    o_rs,
    op_ss,
    op_rs,
):
    row = lax.axis_index("row")
    col = lax.axis_index("col")
    core = lax.rem(row, 2)
    level = lax.div(row, 2)
    n_z = n_row // 2
    own, width = feat_ref.shape
    half = width // 2
    share = cot_ref.shape[0]
    blocks, slots, entries = tgt_ref.shape
    per_block = slots * entries
    chunk = half // n_z
    other_row = row + 1 - 2 * core

    loads = [
        pltpu.make_async_copy(source, target, in_sem.at[index])
        for index, (source, target) in enumerate(
            (
                (feat_hbm, feat_ref),
                (sscale_hbm, sscale_ref),
                (count_hbm, count_ref),
                (slot_hbm, slot_ref),
                (tgt_hbm, tgt_ref),
                (src_hbm, src_ref),
                (tscale_hbm, tscale_ref),
                (weight_hbm, weight_ref),
                (cot_hbm, cot_ref),
            )
        )
    ]
    barrier = pltpu.get_barrier_semaphore()

    def line_peer(step):
        return lax.rem(level + step, n_z)

    def col_peer(step):
        return lax.rem(col + step, n_col)

    def greet(peer_row, peer_col):
        pl.semaphore_signal(
            barrier, 1, device_id=(peer_row, peer_col), device_id_type=pl.DeviceIdType.MESH
        )

    greet(other_row, col)
    each(1, n_z, lambda step: greet(line_peer(step) * 2 + core, col))
    each(1, n_col, lambda step: greet(row, col_peer(step)))
    for load in loads:
        load.start()

    def remote(source, target, send_sem, recv_sem, peer_row, peer_col):
        return pltpu.make_async_remote_copy(
            src_ref=source,
            dst_ref=target,
            send_sem=send_sem,
            recv_sem=recv_sem,
            device_id=(peer_row, peer_col),
            device_id_type=pl.DeviceIdType.MESH,
        )

    def on_line(source, target, send_sem, recv_sem, peer, at):
        return remote(
            source, target(at), send_sem.at[peer], recv_sem.at[at], peer * 2 + core, col
        )

    def on_col(source, target, send_sem, recv_sem, peer, at):
        return remote(source, target.at[at], send_sem.at[peer], recv_sem.at[at], row, peer)

    loads[0].wait()
    loads[1].wait()
    source_col = to_column(lambda part: sscale_ref[pl.ds(part, 1), :], own // B, 0, own)
    scaled = (source_col * feat_ref[...].astype(F32)).astype(BF)
    for part in range(2):
        gath[part, core, level] = scaled[:, part * half : (part + 1) * half]
    pl.semaphore_wait(barrier, n_z + n_col - 1)

    def feat_copy(part, peer, at):
        return on_line(
            gath.at[part, core, level],
            lambda place: gath.at[part, core, place],
            g_ss.at[part],
            g_rs.at[part],
            peer,
            at,
        )

    def feat_pair(part, of_core):
        line = gath.at[part, of_core]
        return remote(line, line, gp_ss.at[part], gp_rs.at[part], other_row, col)

    def send_feat(part):
        each(1, n_z, lambda step: feat_copy(part, line_peer(step), level).start())

    def forward_feat(part):
        def wait(step):
            feat_copy(part, line_peer(step), line_peer(step)).wait()

        each(1, n_z, wait)
        feat_pair(part, core).start()

    send_feat(0)
    for load in loads[2:7]:
        load.wait()

    lane = lax.broadcasted_iota(jnp.int32, (entries, per_block), 1)
    spread = (lane % entries == lax.broadcasted_iota(jnp.int32, (entries, per_block), 0)).astype(
        F32
    ).astype(BF)
    slot_lane = lax.broadcasted_iota(jnp.int32, (slots, per_block), 1) // entries
    slot_hot = slot_lane == lax.broadcasted_iota(jnp.int32, (slots, per_block), 0)

    def flatten(ref):
        flat = ref[...].reshape(blocks * slots, entries).astype(F32).astype(BF)
        wide = dot(flat, spread).reshape(blocks, slots, per_block)
        return jnp.sum(jnp.where(slot_hot[None], wide, 0.0), axis=1)

    block_lane = lax.broadcasted_iota(jnp.int32, (blocks, per_block), 1) // entries
    square = (blocks, blocks)
    diagonal = lax.broadcasted_iota(jnp.int32, square, 0) == lax.broadcasted_iota(
        jnp.int32, square, 1
    )
    counts = jnp.sum(
        jnp.where(diagonal, count_ref[...].astype(F32), 0.0), axis=1, keepdims=True
    )
    alive = block_lane.astype(F32) < counts
    edges[0] = jnp.where(alive, flatten(tgt_ref), -1.0)
    edges[1] = flatten(src_ref)
    edges[2] = dot(slot_ref[...].astype(F32).astype(BF), slot_hot.astype(F32).astype(BF))

    place = lax.broadcasted_iota(jnp.int32, (B, per_block), 0).astype(F32)

    def fill(block, carry):
        target_hot = (place == edges[0, pl.ds(block, 1), :]).astype(F32).astype(BF)
        source_hot = (place == edges[1, pl.ds(block, 1), :]).astype(F32).astype(BF)
        slot_row = edges[2, pl.ds(block, 1), :]
        step = min(8, n_row)
        for begin in range(0, n_row, step):
            parts = []
            for at in range(begin, begin + step):
                source = (at % n_z) * 2 + at // n_z
                here = (slot_row == float(source)).astype(F32).astype(BF)
                parts.append(source_hot * here)
            placed = jnp.concatenate(parts, axis=0)
            span = pl.ds(begin * B, step * B)
            adj[rows_at(block, B), span] = dot(target_hot, placed, NT).astype(BF)
            adj_t[span, rows_at(block, B)] = dot(placed, target_hot, NT).astype(BF)
        return carry

    lax.fori_loop(0, blocks // 2, fill, 0)
    send_feat(1)
    forward_feat(0)
    lax.fori_loop(blocks // 2, blocks, fill, 0)
    scale_share = to_column(
        lambda part: tscale_ref[pl.ds(part, 1), :], blocks, col * share, share
    )

    def part_copy(part, peer, at):
        return on_col(
            part_send.at[part, peer],
            part_recv.at[part],
            p_ss.at[part],
            p_rs.at[part],
            peer,
            at,
        )

    def forward(part):
        feat_pair(part, 1 - core).wait_recv()
        feat_pair(part, core).wait_send()
        gathered = gath[part].reshape(n_row * own, half)

        def send_part(step):
            peer = col_peer(step)
            part_send[part, peer] = dot(adj[rows_at(peer, share), :], gathered).astype(BF)
            part_copy(part, peer, col).start()

        each(1, n_col, send_part)
        part_recv[part, col] = dot(adj[rows_at(col, share), :], gathered).astype(BF)

    forward(0)
    forward_feat(1)
    forward(1)
    loads[7].wait()
    loads[8].wait()

    z_value = jnp.zeros((share, width), F32)
    for part in range(2):
        each(1, n_col, lambda step: part_copy(part, col_peer(step), col_peer(step)).wait())
        summed = jnp.sum(part_recv[part].astype(F32), axis=0)
        agg_part = (scale_share * summed).astype(BF)
        agg[part] = agg_part
        z_value = z_value + dot(agg_part, weight_ref[part * half : (part + 1) * half, :])
    sigma = jax.nn.sigmoid(z_value)
    deriv = sigma * (1.0 + z_value * (1.0 - sigma))
    grad = (cot_ref[...].astype(F32) * deriv).astype(BF)

    def gy_copy(part, peer, at):
        return on_col(
            gy.at[part, col], gy.at[part], y_ss.at[part], y_rs.at[part], peer, at
        )

    for part in range(2):
        rows = weight_ref[part * half : (part + 1) * half, :]
        gy[part, col] = (scale_share * dot(grad, rows, NT)).astype(BF)
        each(1, n_col, lambda step: gy_copy(part, col_peer(step), col).start())

    w_pair[...] = (
        dot(agg[1 - core], grad, TN).reshape(n_z, chunk, width).astype(w_pair.dtype)
    )
    pair_w = remote(w_pair, w_got, wp_ss, wp_rs, other_row, col)
    pair_w.start()
    act_ref[...] = (z_value * sigma).astype(BF)
    mine = dot(agg[core], grad, TN).reshape(n_z, chunk, width)

    def w_copy(peer, at):
        return on_line(
            w_send.at[peer], lambda place: w_recv.at[place], w_ss, w_rs, peer, at
        )

    pair_w.wait()
    w_send[...] = (mine + w_got[...].astype(F32)).astype(w_send.dtype)
    each(1, n_z, lambda step: w_copy(line_peer(step), level).start())
    w_recv[level] = w_send[level]

    def f_pair_copy(part):
        return remote(
            f_pair.at[part], f_got.at[part], fp_ss.at[part], fp_rs.at[part], other_row, col
        )

    def f_copy(part, peer, at):
        return on_line(
            f_send.at[part, peer],
            lambda place: f_recv.at[part, place],
            f_ss.at[part],
            f_rs.at[part],
            peer,
            at,
        )

    def x_copy(peer, at):
        return on_col(x_all.at[col], x_all, x_ss, x_rs, peer, at)

    def o_copy(peer, at):
        return on_line(
            w_all.at[core, level], lambda place: w_all.at[core, place], o_ss, o_rs, peer, at
        )

    for part in range(2):
        each(1, n_col, lambda step: gy_copy(part, col_peer(step), col_peer(step)).wait())
        grad_y = gy[part].reshape(n_col * share, half)
        line = n_z * own
        f_pair[part] = (
            dot(adj_t[rows_at(1 - core, line), :], grad_y).reshape(n_z, own, half).astype(BF)
        )
        f_pair_copy(part).start()
        kept = dot(adj_t[rows_at(core, line), :], grad_y).reshape(n_z, own, half)
        if part == 0:
            each(1, n_z, lambda step: w_copy(line_peer(step), line_peer(step)).wait())
            x_all[col] = jnp.sum(w_recv[...].astype(F32), axis=0).astype(x_all.dtype)
            each(1, n_col, lambda step: x_copy(col_peer(step), col).start())
        f_pair_copy(part).wait()
        f_send[part] = (kept + f_got[part].astype(F32)).astype(BF)
        each(1, n_z, lambda step: f_copy(part, line_peer(step), level).start())
        f_recv[part, level] = f_send[part, level]

    each(1, n_col, lambda step: x_copy(col_peer(step), col_peer(step)).wait())
    w_all[core, level] = (
        jnp.sum(x_all[...].astype(F32), axis=0) * (1.0 / math.sqrt(total_nodes))
    ).astype(w_all.dtype)
    each(1, n_z, lambda step: o_copy(line_peer(step), level).start())

    def pair_o(of_core):
        return remote(w_all.at[of_core], w_all.at[of_core], op_ss, op_rs, other_row, col)

    def finish(part):
        each(1, n_z, lambda step: f_copy(part, line_peer(step), line_peer(step)).wait())
        fgrad_ref[:, part * half : (part + 1) * half] = (
            source_col * jnp.sum(f_recv[part].astype(F32), axis=0)
        ).astype(BF)

    finish(0)
    each(1, n_z, lambda step: o_copy(line_peer(step), line_peer(step)).wait())
    pair_o(core).start()
    finish(1)
    pair_o(1 - core).wait_recv()
    pair_o(core).wait_send()
    wgrad_ref[...] = w_all[...].astype(F32).reshape(wgrad_ref.shape)


def on_device(
    features,
    source_scale,
    target_scale,
    weight,
    cotangent,
    tile_src,
    tile_count,
    edge_tgt,
    edge_src,
    n_row,
    n_col,
):
    own, width = features.shape
    share = cotangent.shape[0]
    blocks, _, slots, entries = edge_tgt.shape
    targets = blocks * B
    sources = own * n_row
    n_z = n_row // 2
    half = width // 2
    chunk = half // n_z
    wtype = BF if chunk % 16 == 0 else F32
    operands = (
        features,
        source_scale.reshape(own // B, B),
        target_scale.reshape(blocks, B),
        weight,
        cotangent,
        tile_src[:, 0],
        tile_count.reshape(1, blocks),
        edge_tgt[:, 0],
        edge_src[:, 0],
    )
    vmem = pl.BlockSpec(memory_space=pltpu.VMEM)
    dma = pltpu.SemaphoreType.DMA
    return pl.pallas_call(
        functools.partial(kernel, n_row, n_col, targets * n_row),
        out_shape=(
            jax.ShapeDtypeStruct((share, width), BF),
            jax.ShapeDtypeStruct((width, width), F32),
            jax.ShapeDtypeStruct((own, width), BF),
        ),
        in_specs=[pl.BlockSpec(memory_space=pltpu.HBM)] * 9,
        out_specs=(vmem,) * 3,
        scratch_shapes=[pltpu.VMEM(item.shape, item.dtype) for item in operands]
        + [
            pltpu.VMEM((2, 2, n_z, own, half), BF),
            pltpu.VMEM((targets, sources), BF),
            pltpu.VMEM((sources, targets), BF),
            pltpu.VMEM((3, blocks, slots * entries), F32),
            pltpu.VMEM((2, n_col, share, half), BF),
            pltpu.VMEM((2, n_col, share, half), BF),
            pltpu.VMEM((2, share, half), BF),
            pltpu.VMEM((2, n_col, share, half), BF),
        ]
        + [pltpu.VMEM((2, n_z, own, half), BF)] * 4
        + [pltpu.VMEM((n_z, chunk, width), wtype)] * 4
        + [
            pltpu.VMEM((n_col, chunk, width), wtype),
            pltpu.VMEM((2, n_z, chunk, width), wtype),
            dma((9,)),
        ]
        + [dma((2, n_z))] * 2
        + [dma((2,))] * 2
        + [dma((2, n_col))] * 4
        + [dma((2,))] * 2
        + [dma((2, n_z))] * 2
        + [dma(())] * 2
        + [dma((n_z,))] * 2
        + [dma((n_col,))] * 2
        + [dma((n_z,))] * 2
        + [dma(())] * 2,
        compiler_params=pltpu.CompilerParams(
            collective_id=0, has_side_effects=True, vmem_limit_bytes=48 * 1024 * 1024
        ),
        cost_estimate=pl.CostEstimate(
            flops=4 * targets * sources * width,
            bytes_accessed=4 * sources * width,
            transcendentals=share * width,
        ),
    )(*operands)


def solution(mesh):
    in_specs = (
        P(("col", "row"), None),
        P(("col", "row")),
        P("row"),
        P(),
        P(("row", "col"), None),
        P("row", "col", None),
        P("row", "col"),
        P("row", "col", None, None),
        P("row", "col", None, None),
    )
    out_specs = (P(("row", "col"), None), P(), P(("col", "row"), None))
    body = functools.partial(on_device, n_row=mesh.shape["row"], n_col=mesh.shape["col"])
    return jax.shard_map(
        body, mesh=mesh, in_specs=in_specs, out_specs=out_specs, check_vma=False
    )
```

```python
import functools
import math

import jax
import jax.numpy as jnp
from jax import lax
from jax.experimental import pallas as pl
from jax.experimental.pallas import tpu as pltpu
from jax.sharding import PartitionSpec as P

B = 128
BF = jnp.bfloat16
F32 = jnp.float32
NN = (((1,), (0,)), ((), ()))
NT = (((1,), (1,)), ((), ()))
TN = (((0,), (0,)), ((), ()))


def dot(left, right, dims=NN):
    return lax.dot_general(left, right, dims, preferred_element_type=F32)


def each(first, last, body):
    if last - first <= 8:
        for index in range(first, last):
            body(index)
    else:
        lax.fori_loop(first, last, lambda index, carry: (body(index), carry)[1], 0)


def rows_at(index, size):
    return pl.ds(pl.multiple_of(index * size, size), size)


def to_column(row_of, parts, offset, rows):
    place = lax.broadcasted_iota(jnp.int32, (rows, B), 0) + offset
    lane = lax.broadcasted_iota(jnp.int32, (rows, B), 1)
    picked = jnp.zeros((rows, B), F32)
    for part in range(parts):
        picked = picked + jnp.where(lane + part * B == place, row_of(part), 0.0)
    return jnp.sum(picked, axis=1, keepdims=True)


def kernel(
    n_row,
    n_col,
    total_nodes,
    feat_hbm,
    sscale_hbm,
    tscale_hbm,
    weight_hbm,
    cot_hbm,
    slot_hbm,
    count_hbm,
    tgt_hbm,
    src_hbm,
    act_hbm,
    wgrad_hbm,
    fgrad_hbm,
    act_ref,
    wgrad_ref,
    fgrad_ref,
    feat_ref,
    sscale_ref,
    tscale_ref,
    weight_ref,
    cot_ref,
    slot_ref,
    count_ref,
    tgt_ref,
    src_ref,
    gath,
    adj,
    adj_t,
    edges,
    part_send,
    part_recv,
    agg,
    gy,
    f_pair,
    f_got,
    f_send,
    f_recv,
    w_pair,
    w_got,
    w_send,
    w_recv,
    x_all,
    w_all,
    in_sem,
    out_sem,
    g_ss,
    g_rs,
    gp_ss,
    gp_rs,
    p_ss,
    p_rs,
    y_ss,
    y_rs,
    fp_ss,
    fp_rs,
    f_ss,
    f_rs,
    wp_ss,
    wp_rs,
    w_ss,
    w_rs,
    x_ss,
    x_rs,
    o_ss,
    o_rs,
    op_ss,
    op_rs,
):
    row = lax.axis_index("row")
    col = lax.axis_index("col")
    core = lax.rem(row, 2)
    level = lax.div(row, 2)
    n_z = n_row // 2
    own, width = feat_ref.shape
    half = width // 2
    share = cot_ref.shape[0]
    blocks, slots, entries = tgt_ref.shape
    per_block = slots * entries
    chunk = half // n_z
    other_row = row + 1 - 2 * core

    loads = [
        pltpu.make_async_copy(source, target, in_sem.at[index])
        for index, (source, target) in enumerate(
            (
                (feat_hbm, feat_ref),
                (sscale_hbm, sscale_ref),
                (count_hbm, count_ref),
                (slot_hbm, slot_ref),
                (tgt_hbm, tgt_ref),
                (src_hbm, src_ref),
                (tscale_hbm, tscale_ref),
                (weight_hbm, weight_ref),
                (cot_hbm, cot_ref),
            )
        )
    ]
    stores = [
        pltpu.make_async_copy(source, target, out_sem.at[index])
        for index, (source, target) in enumerate(
            ((act_ref, act_hbm), (fgrad_ref, fgrad_hbm), (wgrad_ref, wgrad_hbm))
        )
    ]
    barrier = pltpu.get_barrier_semaphore()

    def line_peer(step):
        return lax.rem(level + step, n_z)

    def col_peer(step):
        return lax.rem(col + step, n_col)

    def greet(peer_row, peer_col):
        pl.semaphore_signal(
            barrier, 1, device_id=(peer_row, peer_col), device_id_type=pl.DeviceIdType.MESH
        )

    greet(other_row, col)
    each(1, n_z, lambda step: greet(line_peer(step) * 2 + core, col))
    each(1, n_col, lambda step: greet(row, col_peer(step)))
    for load in loads:
        load.start()

    def remote(source, target, send_sem, recv_sem, peer_row, peer_col):
        return pltpu.make_async_remote_copy(
            src_ref=source,
            dst_ref=target,
            send_sem=send_sem,
            recv_sem=recv_sem,
            device_id=(peer_row, peer_col),
            device_id_type=pl.DeviceIdType.MESH,
        )

    def on_line(source, target, send_sem, recv_sem, peer, at):
        return remote(
            source, target(at), send_sem.at[peer], recv_sem.at[at], peer * 2 + core, col
        )

    def on_col(source, target, send_sem, recv_sem, peer, at):
        return remote(source, target.at[at], send_sem.at[peer], recv_sem.at[at], row, peer)

    loads[0].wait()
    loads[1].wait()
    source_col = to_column(lambda part: sscale_ref[pl.ds(part, 1), :], own // B, 0, own)
    scaled = (source_col * feat_ref[...].astype(F32)).astype(BF)
    for part in range(2):
        gath[part, core, level] = scaled[:, part * half : (part + 1) * half]
    pl.semaphore_wait(barrier, n_z + n_col - 1)

    def feat_copy(part, peer, at):
        return on_line(
            gath.at[part, core, level],
            lambda place: gath.at[part, core, place],
            g_ss.at[part],
            g_rs.at[part],
            peer,
            at,
        )

    def feat_pair(part, of_core):
        line = gath.at[part, of_core]
        return remote(line, line, gp_ss.at[part], gp_rs.at[part], other_row, col)

    def send_feat(part):
        each(1, n_z, lambda step: feat_copy(part, line_peer(step), level).start())

    def forward_feat(part):
        def wait(step):
            feat_copy(part, line_peer(step), line_peer(step)).wait()

        each(1, n_z, wait)
        feat_pair(part, core).start()

    send_feat(0)
    for load in loads[2:7]:
        load.wait()

    lane = lax.broadcasted_iota(jnp.int32, (entries, per_block), 1)
    spread = (lane % entries == lax.broadcasted_iota(jnp.int32, (entries, per_block), 0)).astype(
        F32
    ).astype(BF)
    slot_lane = lax.broadcasted_iota(jnp.int32, (slots, per_block), 1) // entries
    slot_hot = slot_lane == lax.broadcasted_iota(jnp.int32, (slots, per_block), 0)

    def flatten(ref):
        flat = ref[...].reshape(blocks * slots, entries).astype(F32).astype(BF)
        wide = dot(flat, spread).reshape(blocks, slots, per_block)
        return jnp.sum(jnp.where(slot_hot[None], wide, 0.0), axis=1)

    block_lane = lax.broadcasted_iota(jnp.int32, (blocks, per_block), 1) // entries
    square = (blocks, blocks)
    diagonal = lax.broadcasted_iota(jnp.int32, square, 0) == lax.broadcasted_iota(
        jnp.int32, square, 1
    )
    counts = jnp.sum(
        jnp.where(diagonal, count_ref[...].astype(F32), 0.0), axis=1, keepdims=True
    )
    alive = block_lane.astype(F32) < counts
    edges[0] = jnp.where(alive, flatten(tgt_ref), -1.0)
    edges[1] = flatten(src_ref)
    edges[2] = dot(slot_ref[...].astype(F32).astype(BF), slot_hot.astype(F32).astype(BF))

    place = lax.broadcasted_iota(jnp.int32, (B, per_block), 0).astype(F32)

    def fill(block, carry):
        target_hot = (place == edges[0, pl.ds(block, 1), :]).astype(F32).astype(BF)
        source_hot = (place == edges[1, pl.ds(block, 1), :]).astype(F32).astype(BF)
        slot_row = edges[2, pl.ds(block, 1), :]
        step = min(8, n_row)
        for begin in range(0, n_row, step):
            parts = []
            for at in range(begin, begin + step):
                source = (at % n_z) * 2 + at // n_z
                here = (slot_row == float(source)).astype(F32).astype(BF)
                parts.append(source_hot * here)
            placed = jnp.concatenate(parts, axis=0)
            span = pl.ds(begin * B, step * B)
            adj[rows_at(block, B), span] = dot(target_hot, placed, NT).astype(BF)
            adj_t[span, rows_at(block, B)] = dot(placed, target_hot, NT).astype(BF)
        return carry

    lax.fori_loop(0, blocks // 2, fill, 0)
    send_feat(1)
    forward_feat(0)
    lax.fori_loop(blocks // 2, blocks, fill, 0)
    scale_share = to_column(
        lambda part: tscale_ref[pl.ds(part, 1), :], blocks, col * share, share
    )

    def part_copy(part, peer, at):
        return on_col(
            part_send.at[part, peer],
            part_recv.at[part],
            p_ss.at[part],
            p_rs.at[part],
            peer,
            at,
        )

    def forward(part):
        feat_pair(part, 1 - core).wait_recv()
        feat_pair(part, core).wait_send()
        gathered = gath[part].reshape(n_row * own, half)

        def send_part(step):
            peer = col_peer(step)
            part_send[part, peer] = dot(adj[rows_at(peer, share), :], gathered).astype(BF)
            part_copy(part, peer, col).start()

        each(1, n_col, send_part)
        part_recv[part, col] = dot(adj[rows_at(col, share), :], gathered).astype(BF)

    forward(0)
    forward_feat(1)
    forward(1)
    loads[7].wait()
    loads[8].wait()

    z_value = jnp.zeros((share, width), F32)
    for part in range(2):
        each(1, n_col, lambda step: part_copy(part, col_peer(step), col_peer(step)).wait())
        summed = jnp.sum(part_recv[part].astype(F32), axis=0)
        agg_part = (scale_share * summed).astype(BF)
        agg[part] = agg_part
        z_value = z_value + dot(agg_part, weight_ref[part * half : (part + 1) * half, :])
    sigma = jax.nn.sigmoid(z_value)
    deriv = sigma * (1.0 + z_value * (1.0 - sigma))
    grad = (cot_ref[...].astype(F32) * deriv).astype(BF)

    def gy_copy(part, peer, at):
        return on_col(
            gy.at[part, col], gy.at[part], y_ss.at[part], y_rs.at[part], peer, at
        )

    for part in range(2):
        rows = weight_ref[part * half : (part + 1) * half, :]
        gy[part, col] = (scale_share * dot(grad, rows, NT)).astype(BF)
        each(1, n_col, lambda step: gy_copy(part, col_peer(step), col).start())

    w_pair[...] = (
        dot(agg[1 - core], grad, TN).reshape(n_z, chunk, width).astype(w_pair.dtype)
    )
    pair_w = remote(w_pair, w_got, wp_ss, wp_rs, other_row, col)
    pair_w.start()
    act_ref[...] = (z_value * sigma).astype(BF)
    stores[0].start()
    mine = dot(agg[core], grad, TN).reshape(n_z, chunk, width)

    def w_copy(peer, at):
        return on_line(
            w_send.at[peer], lambda place: w_recv.at[place], w_ss, w_rs, peer, at
        )

    pair_w.wait()
    w_send[...] = (mine + w_got[...].astype(F32)).astype(w_send.dtype)
    each(1, n_z, lambda step: w_copy(line_peer(step), level).start())
    w_recv[level] = w_send[level]

    def f_pair_copy(part):
        return remote(
            f_pair.at[part], f_got.at[part], fp_ss.at[part], fp_rs.at[part], other_row, col
        )

    def f_copy(part, peer, at):
        return on_line(
            f_send.at[part, peer],
            lambda place: f_recv.at[part, place],
            f_ss.at[part],
            f_rs.at[part],
            peer,
            at,
        )

    def x_copy(peer, at):
        return on_col(x_all.at[col], x_all, x_ss, x_rs, peer, at)

    def o_copy(peer, at):
        return on_line(
            w_all.at[core, level], lambda place: w_all.at[core, place], o_ss, o_rs, peer, at
        )

    each(1, n_z, lambda step: w_copy(line_peer(step), line_peer(step)).wait())
    x_all[col] = jnp.sum(w_recv[...].astype(F32), axis=0).astype(x_all.dtype)
    each(1, n_col, lambda step: x_copy(col_peer(step), col).start())

    for part in range(2):
        each(1, n_col, lambda step: gy_copy(part, col_peer(step), col_peer(step)).wait())
        grad_y = gy[part].reshape(n_col * share, half)
        line = n_z * own
        f_pair[part] = (
            dot(adj_t[rows_at(1 - core, line), :], grad_y).reshape(n_z, own, half).astype(BF)
        )
        f_pair_copy(part).start()
        kept = dot(adj_t[rows_at(core, line), :], grad_y).reshape(n_z, own, half)
        if part == 1:
            each(1, n_col, lambda step: x_copy(col_peer(step), col_peer(step)).wait())
            w_all[core, level] = (
                jnp.sum(x_all[...].astype(F32), axis=0) * (1.0 / math.sqrt(total_nodes))
            ).astype(w_all.dtype)
            each(1, n_z, lambda step: o_copy(line_peer(step), level).start())
        f_pair_copy(part).wait()
        f_send[part] = (kept + f_got[part].astype(F32)).astype(BF)
        each(1, n_z, lambda step: f_copy(part, line_peer(step), level).start())
        f_recv[part, level] = f_send[part, level]

    def pair_o(of_core):
        return remote(w_all.at[of_core], w_all.at[of_core], op_ss, op_rs, other_row, col)

    def finish(part):
        each(1, n_z, lambda step: f_copy(part, line_peer(step), line_peer(step)).wait())
        fgrad_ref[:, part * half : (part + 1) * half] = (
            source_col * jnp.sum(f_recv[part].astype(F32), axis=0)
        ).astype(BF)

    finish(0)
    each(1, n_z, lambda step: o_copy(line_peer(step), line_peer(step)).wait())
    pair_o(core).start()
    finish(1)
    stores[1].start()
    pair_o(1 - core).wait_recv()
    pair_o(core).wait_send()
    wgrad_ref[...] = w_all[...].astype(F32).reshape(wgrad_ref.shape)
    stores[2].start()
    for store in stores:
        store.wait()


def hand_on(*refs):
    load_sem, store_sem = refs[9:]
    loads = [
        pltpu.make_async_copy(refs[index], refs[6 + index], load_sem.at[index])
        for index in range(3)
    ]
    stores = [
        pltpu.make_async_copy(refs[6 + index], refs[3 + index], store_sem.at[index])
        for index in range(3)
    ]
    for load in loads:
        load.start()
    for load, store in zip(loads, stores):
        load.wait()
        store.start()
    for store in stores:
        store.wait()


def on_device(
    features,
    source_scale,
    target_scale,
    weight,
    cotangent,
    tile_src,
    tile_count,
    edge_tgt,
    edge_src,
    n_row,
    n_col,
):
    own, width = features.shape
    share = cotangent.shape[0]
    blocks, _, slots, entries = edge_tgt.shape
    targets = blocks * B
    sources = own * n_row
    n_z = n_row // 2
    half = width // 2
    chunk = half // n_z
    wtype = BF if chunk % 16 == 0 else F32
    operands = (
        features,
        source_scale.reshape(own // B, B),
        target_scale.reshape(blocks, B),
        weight,
        cotangent,
        tile_src[:, 0],
        tile_count.reshape(1, blocks),
        edge_tgt[:, 0],
        edge_src[:, 0],
    )
    dma = pltpu.SemaphoreType.DMA
    shapes = (
        jax.ShapeDtypeStruct((share, width), BF),
        jax.ShapeDtypeStruct((width, width), F32),
        jax.ShapeDtypeStruct((own, width), BF),
    )
    hbm = pl.BlockSpec(memory_space=pltpu.HBM)
    results = pl.pallas_call(
        functools.partial(kernel, n_row, n_col, targets * n_row),
        out_shape=shapes,
        in_specs=[hbm] * 9,
        out_specs=(hbm,) * 3,
        scratch_shapes=[pltpu.VMEM(item.shape, item.dtype) for item in shapes + operands]
        + [
            pltpu.VMEM((2, 2, n_z, own, half), BF),
            pltpu.VMEM((targets, sources), BF),
            pltpu.VMEM((sources, targets), BF),
            pltpu.VMEM((3, blocks, slots * entries), F32),
            pltpu.VMEM((2, n_col, share, half), BF),
            pltpu.VMEM((2, n_col, share, half), BF),
            pltpu.VMEM((2, share, half), BF),
            pltpu.VMEM((2, n_col, share, half), BF),
        ]
        + [pltpu.VMEM((2, n_z, own, half), BF)] * 4
        + [pltpu.VMEM((n_z, chunk, width), wtype)] * 4
        + [
            pltpu.VMEM((n_col, chunk, width), wtype),
            pltpu.VMEM((2, n_z, chunk, width), wtype),
            dma((9,)),
            dma((3,)),
        ]
        + [dma((2, n_z))] * 2
        + [dma((2,))] * 2
        + [dma((2, n_col))] * 4
        + [dma((2,))] * 2
        + [dma((2, n_z))] * 2
        + [dma(())] * 2
        + [dma((n_z,))] * 2
        + [dma((n_col,))] * 2
        + [dma((n_z,))] * 2
        + [dma(())] * 2,
        compiler_params=pltpu.CompilerParams(
            collective_id=0, has_side_effects=True, vmem_limit_bytes=62 * 1024 * 1024
        ),
        cost_estimate=pl.CostEstimate(
            flops=4 * targets * sources * width,
            bytes_accessed=4 * sources * width,
            transcendentals=share * width,
        ),
    )(*operands)
    return pl.pallas_call(
        hand_on,
        out_shape=shapes,
        in_specs=[hbm] * 3,
        out_specs=(hbm,) * 3,
        scratch_shapes=[pltpu.VMEM(item.shape, item.dtype) for item in shapes]
        + [dma((3,))] * 2,
        compiler_params=pltpu.CompilerParams(vmem_limit_bytes=62 * 1024 * 1024),
    )(*results)


def solution(mesh):
    in_specs = (
        P(("col", "row"), None),
        P(("col", "row")),
        P("row"),
        P(),
        P(("row", "col"), None),
        P("row", "col", None),
        P("row", "col"),
        P("row", "col", None, None),
        P("row", "col", None, None),
    )
    out_specs = (P(("row", "col"), None), P(), P(("col", "row"), None))
    body = functools.partial(on_device, n_row=mesh.shape["row"], n_col=mesh.shape["col"])
    return jax.shard_map(
        body, mesh=mesh, in_specs=in_specs, out_specs=out_specs, check_vma=False
    )
```

```python
import functools
import math

import jax
import jax.numpy as jnp
from jax import lax
from jax.experimental import pallas as pl
from jax.experimental.pallas import tpu as pltpu
from jax.sharding import PartitionSpec as P

B = 128
BF = jnp.bfloat16
F32 = jnp.float32
NN = (((1,), (0,)), ((), ()))
NT = (((1,), (1,)), ((), ()))
TN = (((0,), (0,)), ((), ()))


def dot(left, right, dims=NN):
    return lax.dot_general(left, right, dims, preferred_element_type=F32)


def each(first, last, body):
    if last - first <= 8:
        for index in range(first, last):
            body(index)
    else:
        lax.fori_loop(first, last, lambda index, carry: (body(index), carry)[1], 0)


def rows_at(index, size):
    return pl.ds(pl.multiple_of(index * size, size), size)


def to_column(row_of, parts, offset, rows):
    place = lax.broadcasted_iota(jnp.int32, (rows, B), 0) + offset
    lane = lax.broadcasted_iota(jnp.int32, (rows, B), 1)
    picked = jnp.zeros((rows, B), F32)
    for part in range(parts):
        picked = picked + jnp.where(lane + part * B == place, row_of(part), 0.0)
    return jnp.sum(picked, axis=1, keepdims=True)


def kernel(
    n_row,
    n_col,
    total_nodes,
    feat_hbm,
    sscale_hbm,
    tscale_hbm,
    weight_hbm,
    cot_hbm,
    slot_hbm,
    count_hbm,
    tgt_hbm,
    src_hbm,
    act_hbm,
    wgrad_hbm,
    fgrad_hbm,
    act_ref,
    wgrad_ref,
    fgrad_ref,
    feat_ref,
    sscale_ref,
    tscale_ref,
    weight_ref,
    cot_ref,
    slot_ref,
    count_ref,
    tgt_ref,
    src_ref,
    gath,
    adj,
    adj_t,
    edges,
    part_send,
    part_recv,
    agg,
    gy,
    f_pair,
    f_got,
    f_send,
    f_recv,
    kept,
    w_pair,
    w_got,
    w_send,
    w_recv,
    x_all,
    w_all,
    in_sem,
    out_sem,
    g_ss,
    g_rs,
    gp_ss,
    gp_rs,
    p_ss,
    p_rs,
    y_ss,
    y_rs,
    fp_ss,
    fp_rs,
    f_ss,
    f_rs,
    wp_ss,
    wp_rs,
    w_ss,
    w_rs,
    x_ss,
    x_rs,
    o_ss,
    o_rs,
    op_ss,
    op_rs,
):
    row = lax.axis_index("row")
    col = lax.axis_index("col")
    core = lax.rem(row, 2)
    level = lax.div(row, 2)
    n_z = n_row // 2
    own, width = feat_ref.shape
    half = width // 2
    share = cot_ref.shape[0]
    blocks, slots, entries = tgt_ref.shape
    per_block = slots * entries
    chunk = half // n_z
    other_row = row + 1 - 2 * core

    loads = [
        pltpu.make_async_copy(source, target, in_sem.at[index])
        for index, (source, target) in enumerate(
            (
                (feat_hbm, feat_ref),
                (sscale_hbm, sscale_ref),
                (count_hbm, count_ref),
                (slot_hbm, slot_ref),
                (tgt_hbm, tgt_ref),
                (src_hbm, src_ref),
                (tscale_hbm, tscale_ref),
                (weight_hbm, weight_ref),
                (cot_hbm, cot_ref),
            )
        )
    ]
    stores = [
        pltpu.make_async_copy(source, target, out_sem.at[index])
        for index, (source, target) in enumerate(
            ((act_ref, act_hbm), (fgrad_ref, fgrad_hbm), (wgrad_ref, wgrad_hbm))
        )
    ]
    barrier = pltpu.get_barrier_semaphore()

    def line_peer(step):
        return lax.rem(level + step, n_z)

    def col_peer(step):
        return lax.rem(col + step, n_col)

    def greet(peer_row, peer_col):
        pl.semaphore_signal(
            barrier, 1, device_id=(peer_row, peer_col), device_id_type=pl.DeviceIdType.MESH
        )

    greet(other_row, col)
    each(1, n_z, lambda step: greet(line_peer(step) * 2 + core, col))
    each(1, n_col, lambda step: greet(row, col_peer(step)))
    for load in loads:
        load.start()

    def remote(source, target, send_sem, recv_sem, peer_row, peer_col):
        return pltpu.make_async_remote_copy(
            src_ref=source,
            dst_ref=target,
            send_sem=send_sem,
            recv_sem=recv_sem,
            device_id=(peer_row, peer_col),
            device_id_type=pl.DeviceIdType.MESH,
        )

    def on_line(source, target, send_sem, recv_sem, peer, at):
        return remote(
            source, target(at), send_sem.at[peer], recv_sem.at[at], peer * 2 + core, col
        )

    def on_col(source, target, send_sem, recv_sem, peer, at):
        return remote(source, target.at[at], send_sem.at[peer], recv_sem.at[at], row, peer)

    loads[0].wait()
    loads[1].wait()
    source_col = to_column(lambda part: sscale_ref[pl.ds(part, 1), :], own // B, 0, own)
    scaled = (source_col * feat_ref[...].astype(F32)).astype(BF)
    for part in range(2):
        gath[part, core, level] = scaled[:, part * half : (part + 1) * half]
    pl.semaphore_wait(barrier, n_z + n_col - 1)

    def feat_copy(part, peer, at):
        return on_line(
            gath.at[part, core, level],
            lambda place: gath.at[part, core, place],
            g_ss.at[part],
            g_rs.at[part],
            peer,
            at,
        )

    def feat_pair(part, of_core):
        line = gath.at[part, of_core]
        return remote(line, line, gp_ss.at[part], gp_rs.at[part], other_row, col)

    def send_feat(part):
        each(1, n_z, lambda step: feat_copy(part, line_peer(step), level).start())

    def forward_feat(part):
        def wait(step):
            feat_copy(part, line_peer(step), line_peer(step)).wait()

        each(1, n_z, wait)
        feat_pair(part, core).start()

    send_feat(0)
    for load in loads[2:7]:
        load.wait()

    lane = lax.broadcasted_iota(jnp.int32, (entries, per_block), 1)
    spread = (lane % entries == lax.broadcasted_iota(jnp.int32, (entries, per_block), 0)).astype(
        F32
    ).astype(BF)
    slot_lane = lax.broadcasted_iota(jnp.int32, (slots, per_block), 1) // entries
    slot_hot = slot_lane == lax.broadcasted_iota(jnp.int32, (slots, per_block), 0)

    def flatten(ref):
        flat = ref[...].reshape(blocks * slots, entries).astype(F32).astype(BF)
        wide = dot(flat, spread).reshape(blocks, slots, per_block)
        return jnp.sum(jnp.where(slot_hot[None], wide, 0.0), axis=1)

    block_lane = lax.broadcasted_iota(jnp.int32, (blocks, per_block), 1) // entries
    square = (blocks, blocks)
    diagonal = lax.broadcasted_iota(jnp.int32, square, 0) == lax.broadcasted_iota(
        jnp.int32, square, 1
    )
    counts = jnp.sum(
        jnp.where(diagonal, count_ref[...].astype(F32), 0.0), axis=1, keepdims=True
    )
    alive = block_lane.astype(F32) < counts
    edges[0] = jnp.where(alive, flatten(tgt_ref), -1.0)
    edges[1] = flatten(src_ref)
    edges[2] = dot(slot_ref[...].astype(F32).astype(BF), slot_hot.astype(F32).astype(BF))

    place = lax.broadcasted_iota(jnp.int32, (B, per_block), 0).astype(F32)

    def fill(block, carry):
        target_hot = (place == edges[0, pl.ds(block, 1), :]).astype(F32).astype(BF)
        source_hot = (place == edges[1, pl.ds(block, 1), :]).astype(F32).astype(BF)
        slot_row = edges[2, pl.ds(block, 1), :]
        step = min(8, n_row)
        for begin in range(0, n_row, step):
            parts = []
            for at in range(begin, begin + step):
                source = (at % n_z) * 2 + at // n_z
                here = (slot_row == float(source)).astype(F32).astype(BF)
                parts.append(source_hot * here)
            placed = jnp.concatenate(parts, axis=0)
            span = pl.ds(begin * B, step * B)
            adj[rows_at(block, B), span] = dot(target_hot, placed, NT).astype(BF)
            adj_t[span, rows_at(block, B)] = dot(placed, target_hot, NT).astype(BF)
        return carry

    lax.fori_loop(0, blocks // 2, fill, 0)
    send_feat(1)
    forward_feat(0)
    lax.fori_loop(blocks // 2, blocks, fill, 0)
    scale_share = to_column(
        lambda part: tscale_ref[pl.ds(part, 1), :], blocks, col * share, share
    )

    def part_copy(part, peer, at):
        return on_col(
            part_send.at[part, peer],
            part_recv.at[part],
            p_ss.at[part],
            p_rs.at[part],
            peer,
            at,
        )

    def forward(part):
        feat_pair(part, 1 - core).wait_recv()
        feat_pair(part, core).wait_send()
        gathered = gath[part].reshape(n_row * own, half)

        def send_part(step):
            peer = col_peer(step)
            part_send[part, peer] = dot(adj[rows_at(peer, share), :], gathered).astype(BF)
            part_copy(part, peer, col).start()

        each(1, n_col, send_part)
        part_recv[part, col] = dot(adj[rows_at(col, share), :], gathered).astype(BF)

    forward(0)
    forward_feat(1)
    forward(1)
    loads[7].wait()
    loads[8].wait()

    z_value = jnp.zeros((share, width), F32)
    for part in range(2):
        each(1, n_col, lambda step: part_copy(part, col_peer(step), col_peer(step)).wait())
        summed = jnp.sum(part_recv[part].astype(F32), axis=0)
        agg_part = (scale_share * summed).astype(BF)
        agg[part] = agg_part
        z_value = z_value + dot(agg_part, weight_ref[part * half : (part + 1) * half, :])
    sigma = jax.nn.sigmoid(z_value)
    deriv = sigma * (1.0 + z_value * (1.0 - sigma))
    grad = (cot_ref[...].astype(F32) * deriv).astype(BF)

    def gy_copy(part, peer, at):
        return on_col(
            gy.at[part, col], gy.at[part], y_ss.at[part], y_rs.at[part], peer, at
        )

    for part in range(2):
        rows = weight_ref[part * half : (part + 1) * half, :]
        gy[part, col] = (scale_share * dot(grad, rows, NT)).astype(BF)
        each(1, n_col, lambda step: gy_copy(part, col_peer(step), col).start())

    w_pair[...] = (
        dot(agg[1 - core], grad, TN).reshape(n_z, chunk, width).astype(w_pair.dtype)
    )
    pair_w = remote(w_pair, w_got, wp_ss, wp_rs, other_row, col)
    pair_w.start()
    act_ref[...] = (z_value * sigma).astype(BF)
    stores[0].start()
    mine = dot(agg[core], grad, TN).reshape(n_z, chunk, width)

    def w_copy(peer, at):
        return on_line(
            w_send.at[peer], lambda place: w_recv.at[place], w_ss, w_rs, peer, at
        )

    pair_w.wait()
    w_send[...] = (mine + w_got[...].astype(F32)).astype(w_send.dtype)
    each(1, n_z, lambda step: w_copy(line_peer(step), level).start())
    w_recv[level] = w_send[level]

    def f_pair_copy(part, at):
        return remote(
            f_pair.at[part, at],
            f_got.at[part, at],
            fp_ss.at[part, at],
            fp_rs.at[part, at],
            other_row,
            col,
        )

    def f_copy(part, peer, at):
        return on_line(
            f_send.at[part, peer],
            lambda place: f_recv.at[part, place],
            f_ss.at[part],
            f_rs.at[part],
            peer,
            at,
        )

    def x_copy(peer, at):
        return on_col(x_all.at[col], x_all, x_ss, x_rs, peer, at)

    def o_copy(peer, at):
        return on_line(
            w_all.at[core, level], lambda place: w_all.at[core, place], o_ss, o_rs, peer, at
        )

    each(1, n_z, lambda step: w_copy(line_peer(step), line_peer(step)).wait())
    x_all[col] = jnp.sum(w_recv[...].astype(F32), axis=0).astype(x_all.dtype)
    each(1, n_col, lambda step: x_copy(col_peer(step), col).start())

    for part in range(2):
        each(1, n_col, lambda step: gy_copy(part, col_peer(step), col_peer(step)).wait())
        grad_y = gy[part].reshape(n_col * share, half)

        def product(of_core, at):
            return dot(adj_t[rows_at(of_core * n_z + at, own), :], grad_y)

        def send_pair(step):
            at = line_peer(step)
            f_pair[part, at] = product(1 - core, at).astype(BF)
            f_pair_copy(part, at).start()

        def keep(step):
            at = line_peer(step)
            kept[at] = product(core, at)

        def pass_on(step):
            at = line_peer(step)
            f_pair_copy(part, at).wait()
            total = (kept[at] + f_got[part, at].astype(F32)).astype(BF)
            f_send[part, at] = total
            f_copy(part, at, level).start()

        each(1, n_z + 1, send_pair)
        each(1, n_z + 1, keep)
        if part == 1:
            each(1, n_col, lambda step: x_copy(col_peer(step), col_peer(step)).wait())
            w_all[core, level] = (
                jnp.sum(x_all[...].astype(F32), axis=0) * (1.0 / math.sqrt(total_nodes))
            ).astype(w_all.dtype)
            each(1, n_z, lambda step: o_copy(line_peer(step), level).start())
        each(1, n_z, pass_on)
        f_pair_copy(part, level).wait()
        f_recv[part, level] = (kept[level] + f_got[part, level].astype(F32)).astype(BF)

    def pair_o(of_core):
        return remote(w_all.at[of_core], w_all.at[of_core], op_ss, op_rs, other_row, col)

    def finish(part):
        each(1, n_z, lambda step: f_copy(part, line_peer(step), line_peer(step)).wait())
        fgrad_ref[:, part * half : (part + 1) * half] = (
            source_col * jnp.sum(f_recv[part].astype(F32), axis=0)
        ).astype(BF)

    finish(0)
    each(1, n_z, lambda step: o_copy(line_peer(step), line_peer(step)).wait())
    pair_o(core).start()
    finish(1)
    stores[1].start()
    pair_o(1 - core).wait_recv()
    pair_o(core).wait_send()
    wgrad_ref[...] = w_all[...].astype(F32).reshape(wgrad_ref.shape)
    stores[2].start()
    for store in stores:
        store.wait()


def hand_on(*refs):
    load_sem, store_sem = refs[9:]
    loads = [
        pltpu.make_async_copy(refs[index], refs[6 + index], load_sem.at[index])
        for index in range(3)
    ]
    stores = [
        pltpu.make_async_copy(refs[6 + index], refs[3 + index], store_sem.at[index])
        for index in range(3)
    ]
    for load in loads:
        load.start()
    for load, store in zip(loads, stores):
        load.wait()
        store.start()
    for store in stores:
        store.wait()


def on_device(
    features,
    source_scale,
    target_scale,
    weight,
    cotangent,
    tile_src,
    tile_count,
    edge_tgt,
    edge_src,
    n_row,
    n_col,
):
    own, width = features.shape
    share = cotangent.shape[0]
    blocks, _, slots, entries = edge_tgt.shape
    targets = blocks * B
    sources = own * n_row
    n_z = n_row // 2
    half = width // 2
    chunk = half // n_z
    wtype = BF if chunk % 16 == 0 else F32
    operands = (
        features,
        source_scale.reshape(own // B, B),
        target_scale.reshape(blocks, B),
        weight,
        cotangent,
        tile_src[:, 0],
        tile_count.reshape(1, blocks),
        edge_tgt[:, 0],
        edge_src[:, 0],
    )
    dma = pltpu.SemaphoreType.DMA
    shapes = (
        jax.ShapeDtypeStruct((share, width), BF),
        jax.ShapeDtypeStruct((width, width), F32),
        jax.ShapeDtypeStruct((own, width), BF),
    )
    hbm = pl.BlockSpec(memory_space=pltpu.HBM)
    results = pl.pallas_call(
        functools.partial(kernel, n_row, n_col, targets * n_row),
        out_shape=shapes,
        in_specs=[hbm] * 9,
        out_specs=(hbm,) * 3,
        scratch_shapes=[pltpu.VMEM(item.shape, item.dtype) for item in shapes + operands]
        + [
            pltpu.VMEM((2, 2, n_z, own, half), BF),
            pltpu.VMEM((targets, sources), BF),
            pltpu.VMEM((sources, targets), BF),
            pltpu.VMEM((3, blocks, slots * entries), F32),
            pltpu.VMEM((2, n_col, share, half), BF),
            pltpu.VMEM((2, n_col, share, half), BF),
            pltpu.VMEM((2, share, half), BF),
            pltpu.VMEM((2, n_col, share, half), BF),
        ]
        + [pltpu.VMEM((2, n_z, own, half), BF)] * 4
        + [pltpu.VMEM((n_z, own, half), F32)]
        + [pltpu.VMEM((n_z, chunk, width), wtype)] * 4
        + [
            pltpu.VMEM((n_col, chunk, width), wtype),
            pltpu.VMEM((2, n_z, chunk, width), wtype),
            dma((9,)),
            dma((3,)),
        ]
        + [dma((2, n_z))] * 2
        + [dma((2,))] * 2
        + [dma((2, n_col))] * 4
        + [dma((2, n_z))] * 2
        + [dma((2, n_z))] * 2
        + [dma(())] * 2
        + [dma((n_z,))] * 2
        + [dma((n_col,))] * 2
        + [dma((n_z,))] * 2
        + [dma(())] * 2,
        compiler_params=pltpu.CompilerParams(
            collective_id=0, has_side_effects=True, vmem_limit_bytes=62 * 1024 * 1024
        ),
        cost_estimate=pl.CostEstimate(
            flops=4 * targets * sources * width,
            bytes_accessed=4 * sources * width,
            transcendentals=share * width,
        ),
    )(*operands)
    return pl.pallas_call(
        hand_on,
        out_shape=shapes,
        in_specs=[hbm] * 3,
        out_specs=(hbm,) * 3,
        scratch_shapes=[pltpu.VMEM(item.shape, item.dtype) for item in shapes]
        + [dma((3,))] * 2,
        compiler_params=pltpu.CompilerParams(vmem_limit_bytes=62 * 1024 * 1024),
    )(*results)


def solution(mesh):
    in_specs = (
        P(("col", "row"), None),
        P(("col", "row")),
        P("row"),
        P(),
        P(("row", "col"), None),
        P("row", "col", None),
        P("row", "col"),
        P("row", "col", None, None),
        P("row", "col", None, None),
    )
    out_specs = (P(("row", "col"), None), P(), P(("col", "row"), None))
    body = functools.partial(on_device, n_row=mesh.shape["row"], n_col=mesh.shape["col"])
    return jax.shard_map(
        body, mesh=mesh, in_specs=in_specs, out_specs=out_specs, check_vma=False
    )
```
